32 devices in a mesh: row: 4 (over y, core), col: 8 (over z, x).
Axes of the slice: x: 2, y: 2, z: 4, core: 2. Of those that a mesh axis runs over, the one named last changes fastest.
Arguments:
- a_values: float32 [256, 64, 448], P(('row', 'col')), may hold values from -0.75 to 0.75
- a_columns: int32 [256, 7], P(('row', 'col')), may hold values from 0 to 255, as said below
- p_values: float32 [256, 64, 256], P(('row', 'col')), may hold values from -0.75 to 0.75
- p_columns: int32 [256, 4], P(('row', 'col')), may hold values from 0 to 3
- p_count: int32 [256], P(('row', 'col')), may hold values from 1 to 4
- aggregates: int32 [256], P(('row', 'col')), may hold values from 0 to 3, as said below
Outputs:
- coarse_operator: float32 [128, 64, 1280], P(('row', 'col'))
The draws below stay inside these ranges and needn't reach their ends.
Inputs may be any that keep to these rules, and one draw needn't show every extreme that they name: `a_columns`: slot 0 of each fine block row names that row itself; every slot names a fine block row of the row's own subdomain or of one of its neighbours 1 to 4; repeated columns add. Each of a subdomain's 4 aggregates holds at least one of its fine block rows.
All inputs are finite; a program needn't handle non-finite values.
Results may differ from the reference program's by a relative error of at most 0.0003.
Values sent between devices are 32-bit elements; how exact they have to be, the bound alone decides.
No kernel may reach another device: no remote copies, remote signals or barrier semaphores. Data moves between devices by JAX's collectives and lax.ppermute only.
A program may use at most 64 MiB of HBM per device.

```python
import jax
import jax.numpy as jnp
from jax import lax

BS = 64
KA = 7
KP = 4
CA = 4
FR = 8
NBF = 256
NCA = 128
N_ROW = 4
N_COL = 8


def draw_a_columns(key, part):
    key = jax.random.fold_in(key, 11)
    key_dir, key_local = jax.random.split(key)
    global_row = jnp.arange(NBF, dtype=jnp.int32)
    subdomain = global_row // FR
    local_row = global_row % FR
    grid_row = subdomain // N_COL
    grid_col = subdomain % N_COL
    heading = jax.random.randint(key_dir, (NBF, KA - 1), 0, 5, dtype=jnp.int32)
    forced = (local_row[:, None] < 4) & (jnp.arange(KA - 1, dtype=jnp.int32)[None, :] == 0)
    heading = jnp.where(forced, local_row[:, None] + 1, heading)
    target_row = grid_row[:, None] + jnp.where(heading == 3, -1, jnp.where(heading == 4, 1, 0))
    target_col = (grid_col[:, None] + jnp.where(heading == 1, -1, jnp.where(heading == 2, 1, 0)) + N_COL) % N_COL
    inside = (target_row >= 0) & (target_row < N_ROW)
    target_row = jnp.where(inside, target_row, grid_row[:, None])
    target_col = jnp.where(inside, target_col, grid_col[:, None])
    picked = jax.random.randint(key_local, (NBF, KA - 1), 0, FR, dtype=jnp.int32)
    columns = (target_row * N_COL + target_col) * FR + picked
    return jnp.concatenate([global_row[:, None], columns], axis=1).astype(jnp.int32)


def draw_p_count(key, part):
    key = jax.random.fold_in(key, 12)
    local_row = jnp.arange(NBF, dtype=jnp.int32) % FR
    counts = jax.random.randint(key, (NBF,), 1, KP + 1, dtype=jnp.int32)
    counts = jnp.where(local_row == 0, KP, jnp.where(local_row == 1, 1, counts))
    return counts.astype(jnp.int32)


def draw_aggregates(key, part):
    key = jax.random.fold_in(key, 13)
    key_label, key_offset = jax.random.split(key)
    global_row = jnp.arange(NBF, dtype=jnp.int32)
    local_row = global_row % FR
    subdomain = global_row // FR
    offsets = jax.random.randint(key_offset, (NBF // FR,), 0, CA, dtype=jnp.int32)
    rotated = (local_row + offsets[subdomain]) % CA
    labels = jax.random.randint(key_label, (NBF,), 0, CA, dtype=jnp.int32)
    return jnp.where(local_row < CA, rotated, labels).astype(jnp.int32)


def touch_ends(values, own_key, least, high):
    place = [jax.random.randint(jax.random.fold_in(own_key, axis), (), 0, length) for axis, length in enumerate(values.shape)]
    main_axis = values.shape.index(max(values.shape))
    beside = place[:main_axis] + [(place[main_axis] + 1) % values.shape[main_axis]] + place[main_axis + 1:]
    return values.at[tuple(place)].set(least).at[tuple(beside)].set(high)


def block_scale(rng, shape, cuts, low, largest):
    def one(axis_at, blocks):
        steps = jax.random.uniform(jax.random.fold_in(jax.random.fold_in(rng, 6), axis_at), (blocks,), jnp.float32, low / len(cuts), largest / len(cuts))
        return jnp.repeat(jnp.exp(steps), shape[axis_at] // blocks).reshape((-1,) + (1,) * (len(shape) - axis_at - 1))

    factor_of = one(*cuts[0])
    for cut in cuts[1:]:
        factor_of = factor_of * one(*cut)
    return factor_of


def gaussian(key, extent, scale, limit, cuts=(), kind=jnp.bfloat16):
    values = jax.random.normal(key, extent, jnp.float32) * scale
    if len(cuts) > 0:
        values = block_scale(key, extent, cuts, -0.22, 0.18) * values
    return jnp.clip(values, min=-limit, max=limit).astype(kind)


def setup_inputs(seed: int = 0) -> dict:
    splits = jax.random.split(jax.random.key(seed), 7)
    a_values = gaussian(splits[0], (NBF, BS, KA * BS), 64 ** -0.5, 0.75, ((0, 32),), jnp.float32)
    a_columns = draw_a_columns(jax.random.fold_in(splits[6], 71), 0)
    p_values = gaussian(splits[2], (NBF, BS, KP * BS), 64 ** -0.5, 0.75, ((0, 32),), jnp.float32)
    p_columns = touch_ends(jax.random.randint(splits[3], (NBF, KP), 0, CA), jax.random.fold_in(splits[3], 1), 0, CA - 1).astype(jnp.int32)
    p_count = draw_p_count(jax.random.fold_in(splits[6], 71), 0)
    aggregates = draw_aggregates(jax.random.fold_in(splits[6], 71), 0)
    return {"a_values": a_values, "a_columns": a_columns, "p_values": p_values, "p_columns": p_columns, "p_count": p_count, "aggregates": aggregates}


highest = lax.Precision.HIGHEST


def dense_prolongator(p_values, p_columns, p_count, aggregates):
    row_count = p_values.shape[0]
    blocks = p_values.reshape(row_count, BS, KP, BS)
    live_slot = (jnp.arange(KP, dtype=jnp.int32)[None, :] < p_count[:, None]).astype(jnp.float32)
    slot_select = (p_columns[:, :, None] == jnp.arange(CA, dtype=jnp.int32)[None, None, :]).astype(jnp.float32)
    slot_select = slot_select * live_slot[:, :, None]
    spread = jnp.einsum('ika,ipkq->ipaq', slot_select, blocks, precision=highest)
    tentative = (aggregates[:, None] == jnp.arange(CA, dtype=jnp.int32)[None, :]).astype(jnp.float32)
    spread = spread + tentative[:, None, :, None] * jnp.eye(BS, dtype=jnp.float32)[:, None, :]
    return spread.reshape(row_count, BS, CA * BS)


def group_codes(targets, grid_row, grid_col):
    target_sub = targets // FR
    target_row = target_sub // N_COL
    target_col = target_sub % N_COL
    lower_col = (grid_col - 1 + N_COL) % N_COL
    inner = jnp.where(target_col == grid_col, 0, jnp.where(target_col == lower_col, 1, 2))
    return jnp.where(target_row == grid_row - 1, 3, jnp.where(target_row == grid_row + 1, 4, inner)).astype(jnp.int32)


def reference(a_values, a_columns, p_values, p_columns, p_count, aggregates):
    dense_rows = dense_prolongator(p_values, p_columns, p_count, aggregates)

    def per_subdomain(subdomain):
        start = (subdomain * FR).astype(jnp.int32)
        a_rows = lax.dynamic_slice_in_dim(a_values, start, FR, 0)
        targets = lax.dynamic_slice_in_dim(a_columns, start, FR, 0)
        own_rows = lax.dynamic_slice_in_dim(dense_rows, start, FR, 0)
        far_rows = jnp.take(dense_rows, targets, axis=0)
        group_code = group_codes(targets, subdomain // N_COL, subdomain % N_COL)
        group_pick = (group_code[:, :, None] == jnp.arange(5, dtype=jnp.int32)[None, None, :]).astype(jnp.float32)
        blocks = a_rows.reshape(FR, BS, KA, BS)
        products = jnp.einsum('lpkq,lkqy->lkpy', blocks, far_rows, precision=highest)
        grouped = jnp.einsum('lkn,lkpy->lnpy', group_pick, products, precision=highest)
        coarse = jnp.einsum('lpx,lnpy->xny', own_rows, grouped, precision=highest)
        return coarse.reshape(CA, BS, 5 * CA * BS)

    result = lax.map(per_subdomain, jnp.arange(N_ROW * N_COL, dtype=jnp.int32))
    return result.reshape(NCA, BS, 5 * CA * BS)
```

```python
import functools

import jax
import jax.numpy as jnp
from jax import lax
from jax.experimental import pallas as pl
from jax.experimental.pallas import tpu as pltpu
from jax.sharding import PartitionSpec as P

BS = 64
KA = 7
KP = 4
CA = 4
WIDE = CA * BS
PARTS = 4

OWN, PAIR_COL, FAR_COL, PAIR_ROW, FAR_ROW = range(5)

VMEM = pl.BlockSpec(memory_space=pltpu.VMEM)
SMEM = pl.BlockSpec(memory_space=pltpu.SMEM)
ANY = pl.BlockSpec(memory_space=pl.ANY)


def split(value):
    high = value.astype(jnp.bfloat16)
    low = (value - high.astype(jnp.float32)).astype(jnp.bfloat16)
    return high, low


def dense_row(row, values, columns_ref, count_ref, aggregates_ref):
    lane = lax.broadcasted_iota(jnp.int32, (1, 2 * BS), 1)
    lower = lane < BS
    diagonal = (
        lax.broadcasted_iota(jnp.int32, (BS, 2 * BS), 0)
        == lax.broadcasted_iota(jnp.int32, (BS, 2 * BS), 1) % BS
    ).astype(jnp.float32)
    live = count_ref[row]
    feeds = [jnp.where(k < live, columns_ref[row, k], -1) for k in range(KP)]
    pieces = []
    for m in range(KP // 2):
        straight = values[:, m * 2 * BS : (m + 1) * 2 * BS]
        pieces.append((jnp.where(lower, feeds[2 * m], feeds[2 * m + 1]), straight))
        pieces.append(
            (jnp.where(lower, feeds[2 * m + 1], feeds[2 * m]), pltpu.roll(straight, BS, 1))
        )
    columns = []
    for j in range(CA // 2):
        wanted = jnp.where(lower, 2 * j, 2 * j + 1)
        total = jnp.where(wanted == aggregates_ref[row], diagonal, 0.0)
        for feed, piece in pieces:
            total = total + jnp.where(feed == wanted, piece, 0.0)
        columns.append(total)
    return jnp.concatenate(columns, axis=1)


def dense_kernel(first, columns_ref, count_ref, aggregates_ref, values_ref, *out_refs):
    for index in range(values_ref.shape[0]):
        row = first + index
        dense = dense_row(row, values_ref[index], columns_ref, count_ref, aggregates_ref)
        if len(out_refs) == 1:
            out_refs[0][index] = dense
        else:
            rows = out_refs[1].shape[0]
            out_refs[0][index] = dense
            if index >= rows:
                out_refs[index // rows][index % rows] = dense


def dense_first(values, columns, count, aggregates, rows):
    return pl.pallas_call(
        functools.partial(dense_kernel, 0),
        grid=(1,),
        in_specs=[SMEM, SMEM, SMEM, pl.BlockSpec((rows, BS, WIDE), lambda i: (0, 0, 0))],
        out_specs=pl.BlockSpec((rows, BS, WIDE), lambda i: (0, 0, 0)),
        out_shape=jax.ShapeDtypeStruct((rows, BS, WIDE), jnp.float32),
        cost_estimate=pl.CostEstimate(flops=100000, bytes_accessed=rows * BS * WIDE * 8, transcendentals=0),
        name="dense_first",
    )(columns, count, aggregates, values)


def dense_all(values, columns, count, aggregates, rows):
    every = values.shape[0]
    shapes = [jax.ShapeDtypeStruct((every, BS, WIDE), jnp.float32)]
    shapes += [jax.ShapeDtypeStruct((rows, BS, WIDE), jnp.float32)] * (every // rows - 1)
    return pl.pallas_call(
        functools.partial(dense_kernel, 0),
        in_specs=[SMEM, SMEM, SMEM, VMEM],
        out_specs=[VMEM] * len(shapes),
        out_shape=shapes,
        cost_estimate=pl.CostEstimate(flops=400000, bytes_accessed=every * BS * WIDE * 12, transcendentals=0),
        name="dense_all",
    )(columns, count, aggregates, values)


def put_block(group, block_ref, out_ref, sem):
    at = pl.multiple_of(group * WIDE, WIDE)
    copy = pltpu.make_async_copy(block_ref, out_ref.at[:, :, pl.ds(at, WIDE)], sem)
    copy.start()
    return copy


def product(high, low, other):
    other_high, other_low = split(other)
    dot = functools.partial(jnp.dot, preferred_element_type=jnp.float32)
    return dot(high, other_high) + (dot(high, other_low) + dot(low, other_high))


def left_kernel(col_count, columns_ref, dense_ref, a_ref, out_ref, high_ref, low_ref, left, block, sem):
    rows = a_ref.shape[0]
    grid_row = lax.axis_index("row")
    grid_col = lax.axis_index("col")
    left[...] = jnp.zeros_like(left)
    for row in range(rows):
        a_high, a_low = split(a_ref[row])
        p_high, p_low = split(dense_ref[row])
        term = lax.dot_general(
            jnp.concatenate([a_high, a_low, a_high], axis=0),
            jnp.concatenate([p_high, p_high, p_low], axis=0),
            (((0,), (0,)), ((), ())),
            preferred_element_type=jnp.float32,
        )
        for slot in range(KA):
            target = columns_ref[row, slot]
            sub = target // rows
            sub_row = sub // col_count
            sub_col = sub - sub_row * col_count
            along = jnp.where(sub_col == grid_col, OWN, jnp.where(sub_col == (grid_col ^ 1), PAIR_COL, FAR_COL))
            across = jnp.where(sub_row == (grid_row ^ 1), PAIR_ROW, FAR_ROW)
            group = jnp.where(sub_row == grid_row, along, across)
            at = pl.multiple_of((group * rows + (target - sub * rows)) * BS, BS)
            left[pl.ds(at, BS), :] += term[slot * BS : (slot + 1) * BS]
    depth = rows * BS
    for group in range(5):
        high, low = split(left[group * depth : (group + 1) * depth, :].T)
        high_ref[group] = high
        low_ref[group] = low
    own = product(high_ref[OWN], low_ref[OWN], dense_ref[...].reshape(depth, WIDE))
    block[...] = own.reshape(CA, BS, WIDE)
    put_block(0, block, out_ref, sem).wait()


def left_parts(a_columns, dense, a_values, col_count):
    rows = a_values.shape[0]
    depth = rows * BS
    return pl.pallas_call(
        functools.partial(left_kernel, col_count),
        in_specs=[SMEM, VMEM, VMEM],
        out_specs=[ANY, VMEM, VMEM],
        out_shape=[
            jax.ShapeDtypeStruct((CA, BS, 5 * WIDE), jnp.float32),
            jax.ShapeDtypeStruct((5, WIDE, depth), jnp.bfloat16),
            jax.ShapeDtypeStruct((5, WIDE, depth), jnp.bfloat16),
        ],
        scratch_shapes=[
            pltpu.VMEM((5 * depth, WIDE), jnp.float32),
            pltpu.VMEM((CA, BS, WIDE), jnp.float32),
            pltpu.SemaphoreType.DMA,
        ],
        compiler_params=pltpu.CompilerParams(vmem_limit_bytes=32 * 1024 * 1024),
        cost_estimate=pl.CostEstimate(flops=2 * 3 * 100000000, bytes_accessed=8000000, transcendentals=0),
        name="left_parts",
    )(a_columns, dense, a_values)


def groups_here():
    col_odd = lax.axis_index("col") % 2
    row_odd = lax.axis_index("row") % 2
    return {PAIR_COL: 2 - col_odd, FAR_COL: 1 + col_odd, PAIR_ROW: 4 - row_odd, FAR_ROW: 3 + row_odd}


def whole_kernel(places, out_in_ref, *refs):
    count = len(places)
    w_refs, far_refs = refs[: 2 * count], refs[2 * count : 3 * count]
    out_ref, blocks, sems = refs[3 * count :]
    del out_in_ref
    groups = groups_here()
    copies = []
    for index, place in enumerate(places):
        depth = w_refs[2 * index].shape[2]
        far = far_refs[index][...].reshape(depth, WIDE)
        term = product(w_refs[2 * index][0], w_refs[2 * index + 1][0], far)
        blocks[index] = term.reshape(CA, BS, WIDE)
        copies.append(put_block(groups[place], blocks.at[index], out_ref, sems.at[index]))
    for copy in copies:
        copy.wait()


def whole_products(out, high, low, fars, places):
    depth = high.shape[2]
    pick = [pl.BlockSpec((1, WIDE, depth), lambda i, place=place: (place, 0, 0)) for place in places]
    return pl.pallas_call(
        functools.partial(whole_kernel, places),
        grid=(1,),
        in_specs=[ANY] + [spec for spec in pick for _ in range(2)] + [pl.BlockSpec(far.shape, lambda i: (0, 0, 0)) for far in fars],
        out_specs=ANY,
        out_shape=jax.ShapeDtypeStruct(out.shape, out.dtype),
        scratch_shapes=[
            pltpu.VMEM((len(places), CA, BS, WIDE), jnp.float32),
            pltpu.SemaphoreType.DMA((len(places),)),
        ],
        input_output_aliases={0: 0},
        compiler_params=pltpu.CompilerParams(vmem_limit_bytes=32 * 1024 * 1024),
        cost_estimate=pl.CostEstimate(flops=len(places) * 3 * 67000000, bytes_accessed=2000000 * len(places), transcendentals=0),
        name="whole_products",
    )(out, *[w for _ in places for w in (high, low)], *fars)


def parts_kernel(place, start, last, out_in_ref, high_ref, low_ref, *refs):
    out_ref, block, sem = refs[-3:]
    del out_in_ref
    part_refs = refs[:-3]
    if start:
        part_refs, before_ref = part_refs[:-1], part_refs[-1]
        total = before_ref[...]
    else:
        total = None
    for index, part_ref in enumerate(part_refs):
        depth = part_ref.shape[0] * BS
        at = index * depth
        term = product(
            high_ref[0, :, at : at + depth], low_ref[0, :, at : at + depth], part_ref[...].reshape(depth, WIDE)
        )
        total = term if total is None else total + term
    block[...] = total.reshape(CA, BS, WIDE)
    put_block(groups_here()[place], block, out_ref, sem).wait()


def parts_product(out, high, low, parts, place):
    depth = high.shape[2]
    w_spec = pl.BlockSpec((1, WIDE, depth), lambda i: (place, 0, 0))
    return pl.pallas_call(
        functools.partial(parts_kernel, place, False, True),
        grid=(1,),
        in_specs=[ANY, w_spec, w_spec] + [pl.BlockSpec(part.shape, lambda i: (0, 0, 0)) for part in parts],
        out_specs=ANY,
        out_shape=jax.ShapeDtypeStruct(out.shape, out.dtype),
        scratch_shapes=[pltpu.VMEM((CA, BS, WIDE), jnp.float32), pltpu.SemaphoreType.DMA],
        input_output_aliases={0: 0},
        compiler_params=pltpu.CompilerParams(vmem_limit_bytes=32 * 1024 * 1024),
        cost_estimate=pl.CostEstimate(flops=3 * 67000000, bytes_accessed=2000000, transcendentals=0),
        name="parts_product",
    )(out, high, low, *parts)


def partial_kernel(high_ref, low_ref, *refs):
    total = None
    for index, part_ref in enumerate(refs[:-1]):
        depth = part_ref.shape[0] * BS
        at = index * depth
        term = product(
            high_ref[0, :, at : at + depth], low_ref[0, :, at : at + depth], part_ref[...].reshape(depth, WIDE)
        )
        total = term if total is None else total + term
    refs[-1][...] = total.reshape(CA, BS, WIDE)


def partial_product(high, low, parts, place):
    depth = sum(part.shape[0] * BS for part in parts)
    w_spec = pl.BlockSpec((1, WIDE, depth), lambda i: (place, 0, 0))
    return pl.pallas_call(
        partial_kernel,
        grid=(1,),
        in_specs=[w_spec, w_spec] + [pl.BlockSpec(part.shape, lambda i: (0, 0, 0)) for part in parts],
        out_specs=pl.BlockSpec((CA, BS, WIDE), lambda i: (0, 0, 0)),
        out_shape=jax.ShapeDtypeStruct((CA, BS, WIDE), jnp.float32),
        compiler_params=pltpu.CompilerParams(vmem_limit_bytes=32 * 1024 * 1024),
        cost_estimate=pl.CostEstimate(flops=3 * 50000000, bytes_accessed=1500000, transcendentals=0),
        name="partial_product",
    )(high, low, *parts)


def last_kernel(place, out_in_ref, high_ref, low_ref, before_ref, part_ref, out_ref, block, sem):
    del out_in_ref
    depth = part_ref.shape[0] * BS
    term = product(high_ref[0], low_ref[0], part_ref[...].reshape(depth, WIDE))
    block[...] = before_ref[...] + term.reshape(CA, BS, WIDE)
    put_block(groups_here()[place], block, out_ref, sem).wait()


def last_product(out, high, low, before, part, place, index):
    depth = part.shape[0] * BS
    w_spec = pl.BlockSpec((1, WIDE, depth), lambda i: (place, 0, index))
    return pl.pallas_call(
        functools.partial(last_kernel, place),
        grid=(1,),
        in_specs=[
            ANY,
            w_spec,
            w_spec,
            pl.BlockSpec(before.shape, lambda i: (0, 0, 0)),
            pl.BlockSpec(part.shape, lambda i: (0, 0, 0)),
        ],
        out_specs=ANY,
        out_shape=jax.ShapeDtypeStruct(out.shape, out.dtype),
        scratch_shapes=[pltpu.VMEM((CA, BS, WIDE), jnp.float32), pltpu.SemaphoreType.DMA],
        input_output_aliases={0: 0},
        cost_estimate=pl.CostEstimate(flops=3 * 17000000, bytes_accessed=700000, transcendentals=0),
        name="last_product",
    )(out, high, low, before, part)


def column_pairs(count):
    return [(i, i ^ 1) for i in range(count)]


def column_onward(count):
    return [(i, ((i ^ 1) + 1) % count if (i ^ 1) % 2 else ((i ^ 1) - 1) % count) for i in range(count)]


def row_pairs(count):
    return [(i, i ^ 1) for i in range(count)]


def row_between(count):
    pairs = [(i, i + 1) for i in range(1, count - 1, 2)]
    return pairs + [(b, a) for a, b in pairs]


def per_device(a_values, a_columns, p_values, p_columns, p_count, aggregates):
    rows = a_values.shape[0] // PARTS
    row_count = lax.axis_size("row")
    col_count = lax.axis_size("col")
    first = dense_first(p_values, p_columns, p_count, aggregates, rows)
    dense, *rest = dense_all(p_values, p_columns, p_count, aggregates, rows)
    pair = [lax.ppermute(part, "col", column_pairs(col_count)) for part in [first, *rest]]
    pair_row = lax.ppermute(dense, "row", row_pairs(row_count))
    far_row = lax.ppermute(dense, "row", row_between(row_count))
    far = [lax.ppermute(part, "col", column_onward(col_count)) for part in pair]
    out, high, low = left_parts(a_columns, dense, a_values, col_count)
    out = whole_products(out, high, low, [pair_row, far_row], (PAIR_ROW, FAR_ROW))
    out = parts_product(out, high, low, pair, PAIR_COL)
    before = partial_product(high, low, far[:-1], FAR_COL)
    return last_product(out, high, low, before, far[-1], FAR_COL, PARTS - 1)


def solution(mesh):
    in_specs = (
        P(("row", "col"), None, None),
        P(("row", "col"), None),
        P(("row", "col"), None, None),
        P(("row", "col"), None),
        P(("row", "col")),
        P(("row", "col")),
    )
    out_specs = P(("row", "col"), None, None)
    return jax.shard_map(
        per_device, mesh=mesh, in_specs=in_specs, out_specs=out_specs, check_vma=False
    )
```

```python
import functools

import jax
import jax.numpy as jnp
from jax import lax
from jax.experimental import pallas as pl
from jax.experimental.pallas import tpu as pltpu
from jax.sharding import PartitionSpec as P

CFG = {'parts': (3, 3, 2), 'xg': 0, 'la': None, 'tick': 1, 'ck': 100000000, 'gk': (2,), 'gf': (), 'rg': None, 'rs': 1, 'pr': 2, 'ch': 1, 'cl': 100000000000, 'ct': 1000000000, 'cp': 100000000, 'ca': 1000, 'cz': 1000, 'cut': 8, 'lb': None, 'g1': []}

BS = 64
KA = 7
KP = 4
CA = 4
WIDE = CA * BS
PARTS = CFG['parts']

OWN, PAIR_COL, FAR_COL, PAIR_ROW, FAR_ROW = range(5)

VMEM = pl.BlockSpec(memory_space=pltpu.VMEM)
HBM = pl.BlockSpec(memory_space=pltpu.HBM)
MIB = 1024 * 1024


def split(value):
    high = value.astype(jnp.bfloat16)
    low = (value - high.astype(jnp.float32)).astype(jnp.bfloat16)
    return high, low


def product(high, low, other):
    other_high, other_low = split(other)
    dot = functools.partial(jnp.dot, preferred_element_type=jnp.float32)
    return dot(high, other_high) + (dot(high, other_low) + dot(low, other_high))


def in_hbm(value):
    return pltpu.with_memory_space_constraint(value, pltpu.HBM)


def in_vmem(value):
    return pltpu.with_memory_space_constraint(value, pltpu.VMEM)


def cost(flops, moved):
    return pl.CostEstimate(flops=flops, bytes_accessed=moved, transcendentals=0)


def dense_row(row, values, columns, counts, aggregates):
    lane = lax.broadcasted_iota(jnp.int32, (1, 2 * BS), 1)
    lower = lane < BS
    diagonal = (
        lax.broadcasted_iota(jnp.int32, (BS, 2 * BS), 0)
        == lax.broadcasted_iota(jnp.int32, (BS, 2 * BS), 1) % BS
    ).astype(jnp.float32)
    live = counts[row]
    feeds = [jnp.where(k < live, columns[k, row], -1) for k in range(KP)]
    pieces = []
    for m in range(KP // 2):
        straight = values[:, m * 2 * BS : (m + 1) * 2 * BS]
        pieces.append((jnp.where(lower, feeds[2 * m], feeds[2 * m + 1]), straight))
        pieces.append(
            (jnp.where(lower, feeds[2 * m + 1], feeds[2 * m]), pltpu.roll(straight, BS, 1))
        )
    dense = []
    for j in range(CA // 2):
        wanted = jnp.where(lower, 2 * j, 2 * j + 1)
        total = jnp.where(wanted == aggregates[row], diagonal, 0.0)
        for feed, piece in pieces:
            total = total + jnp.where(feed == wanted, piece, 0.0)
        dense.append(total)
    return jnp.concatenate(dense, axis=1)


def dense_kernel(values_ref, columns_ref, counts_ref, aggregates_ref, *refs):
    count = len(PARTS)
    part_refs = refs[:count]
    dense_ref, values, columns, counts, aggregates, sems = refs[count:]
    small = [
        pltpu.make_async_copy(source, target, sems.at[index])
        for index, (source, target) in enumerate(
            [(columns_ref, columns), (counts_ref, counts), (aggregates_ref, aggregates)]
        )
    ]
    spans = [pl.ds(sum(PARTS[:part]), PARTS[part]) for part in range(count)]
    large = [
        pltpu.make_async_copy(values_ref.at[span], values.at[span], sems.at[3 + part])
        for part, span in enumerate(spans)
    ]
    for copy in small + large:
        copy.start()
    for copy in small:
        copy.wait()
    for part in range(count):
        large[part].wait()
        for index in range(PARTS[part]):
            row = sum(PARTS[:part]) + index
            dense = dense_row(row, values[row], columns, counts, aggregates)
            part_refs[part][index] = dense
            dense_ref[row] = dense


def dense_rows(p_values, p_columns, p_count, aggregates):
    every = p_values.shape[0]
    *parts, dense = pl.pallas_call(
        dense_kernel,
        in_specs=[HBM] * 4,
        out_specs=[VMEM] * (len(PARTS) + 1),
        out_shape=[pltpu.VMEM((rows, BS, WIDE), jnp.float32) for rows in (*PARTS, every)],
        scratch_shapes=[
            pltpu.VMEM(p_values.shape, jnp.float32),
            pltpu.SMEM((KP, every), jnp.int32),
            pltpu.SMEM((every,), jnp.int32),
            pltpu.SMEM((every,), jnp.int32),
            pltpu.SemaphoreType.DMA((3 + len(PARTS),)),
        ],
        cost_estimate=cost(400000, p_values.size * 12),
        name="dense_rows",
    )(in_hbm(p_values), in_hbm(p_columns.T), in_hbm(p_count), in_hbm(aggregates))
    return parts, dense


def put_block(group, block_ref, out_ref, sem):
    at = pl.multiple_of(group * WIDE, WIDE)
    copy = pltpu.make_async_copy(block_ref, out_ref.at[:, :, pl.ds(at, WIDE)], sem)
    copy.start()
    return copy


def left_kernel(col_count, first, dense_ref, columns_ref, a_ref, *refs):
    left, a, columns, sems = refs[-4:]
    rows = dense_ref.shape[0]
    mine = a.shape[0]
    grid_row = lax.axis_index("row")
    grid_col = lax.axis_index("col")
    small = pltpu.make_async_copy(columns_ref, columns, sems.at[0])
    small.start()
    large = [pltpu.make_async_copy(a_ref.at[first + row], a.at[row], sems.at[1 + row]) for row in range(mine)]
    for copy in large:
        copy.start()
    if first == 0:
        left[...] = jnp.zeros_like(left)
    for copy in large:
        copy.wait()
    small.wait()
    for index in range(mine):
        row = first + index
        a_high, a_low = split(a[index])
        p_high, p_low = split(dense_ref[row])
        turned_a = jnp.concatenate([a_high, a_low], axis=0).T
        term = jnp.dot(
            jnp.concatenate([turned_a, turned_a], axis=1),
            jnp.concatenate([p_high, p_high, p_low, p_low], axis=0),
            preferred_element_type=jnp.float32,
        )
        for slot in range(KA):
            target = columns[row, slot]
            sub = target // rows
            sub_row = sub // col_count
            sub_col = sub - sub_row * col_count
            along = jnp.where(sub_col == grid_col, OWN, jnp.where(sub_col == (grid_col ^ 1), PAIR_COL, FAR_COL))
            across = jnp.where(sub_row == (grid_row ^ 1), PAIR_ROW, FAR_ROW)
            group = jnp.where(sub_row == grid_row, along, across)
            at = pl.multiple_of((group * rows + (target - sub * rows)) * BS, BS)
            left[pl.ds(at, BS), :] += term[slot * BS : (slot + 1) * BS]


def left_product(dense, a_columns, a_values, before, first, count, col_count):
    rows = a_values.shape[0]
    given = [] if before is None else [before]
    return pl.pallas_call(
        functools.partial(left_kernel, col_count, first),
        in_specs=[VMEM, HBM, HBM] + [VMEM] * len(given),
        out_specs=VMEM,
        out_shape=pltpu.VMEM((5 * rows * BS, WIDE), jnp.float32),
        scratch_shapes=[
            pltpu.VMEM((count, *a_values.shape[1:]), jnp.float32),
            pltpu.SMEM(a_columns.shape, jnp.int32),
            pltpu.SemaphoreType.DMA((1 + count,)),
        ],
        input_output_aliases={3: 0} if given else {},
        compiler_params=pltpu.CompilerParams(vmem_limit_bytes=16 * MIB),
        cost_estimate=cost(CFG['cl'], 4000),
        name="left_product",
    )(in_vmem(dense), in_hbm(a_columns), in_hbm(a_values), *map(in_vmem, given))


def turn_kernel(left_ref, high_ref, low_ref):
    depth = high_ref.shape[2]
    for place in range(5):
        high_ref[place], low_ref[place] = split(left_ref[place * depth : (place + 1) * depth, :].T)


def turned(left):
    depth = left.shape[0] // 5
    return pl.pallas_call(
        turn_kernel,
        in_specs=[VMEM],
        out_specs=[VMEM, VMEM],
        out_shape=[pltpu.VMEM((5, WIDE, depth), jnp.bfloat16)] * 2,
        compiler_params=pltpu.CompilerParams(vmem_limit_bytes=16 * MIB),
        cost_estimate=cost(CFG['ct'], 5000),
        name="turned",
    )(in_vmem(left))


def groups_here():
    col_odd = lax.axis_index("col") % 2
    row_odd = lax.axis_index("row") % 2
    return {OWN: 0, PAIR_COL: 2 - col_odd, FAR_COL: 1 + col_odd, PAIR_ROW: 4 - row_odd, FAR_ROW: 3 + row_odd}


def summed(high_ref, low_ref, place, part_refs, at=0):
    total = None
    for part_ref in part_refs:
        depth = part_ref.shape[0] * BS
        term = product(
            high_ref[place, :, at : at + depth], low_ref[place, :, at : at + depth], part_ref[...].reshape(depth, WIDE)
        )
        total = term if total is None else total + term
        at += depth
    return total.reshape(CA, BS, WIDE)


def products_kernel(places, counts, given, *refs):
    high_ref, low_ref, *refs = refs[given:]
    part_refs = refs[: sum(counts)]
    out_ref, blocks, sems = refs[sum(counts) :]
    groups = groups_here()
    copies = []
    for index, place in enumerate(places):
        at = sum(counts[:index])
        blocks[index] = summed(high_ref, low_ref, place, part_refs[at : at + counts[index]])
        copies.append(put_block(groups[place], blocks.at[index], out_ref, sems.at[index]))
    for copy in copies:
        copy.wait()


def products(out, high, low, parts):
    places = tuple(parts)
    counts = tuple(len(parts[place]) for place in places)
    flat = [part for place in places for part in parts[place]]
    given = [] if out is None else [out]
    return pl.pallas_call(
        functools.partial(products_kernel, places, counts, len(given)),
        in_specs=[HBM] * len(given) + [VMEM] * (2 + len(flat)),
        out_specs=HBM,
        out_shape=jax.ShapeDtypeStruct((CA, BS, 5 * WIDE), jnp.float32),
        scratch_shapes=[
            pltpu.VMEM((len(places), CA, BS, WIDE), jnp.float32),
            pltpu.SemaphoreType.DMA((len(places),)),
        ],
        input_output_aliases={0: 0} if given else {},
        compiler_params=pltpu.CompilerParams(vmem_limit_bytes=16 * MIB),
        cost_estimate=cost(CFG['cp'] * len(places), 2000),
        name="products",
    )(*given, *map(in_vmem, (high, low, *flat)))


def partial_kernel(place, at, chained, high_ref, low_ref, *refs):
    part_refs = refs[:-1]
    if chained:
        before_ref, *part_refs = part_refs
        refs[-1][...] = before_ref[...] + summed(high_ref, low_ref, place, part_refs, at)
    else:
        refs[-1][...] = summed(high_ref, low_ref, place, part_refs, at)


def partial_product(high, low, before, parts, place, at):
    given = [] if before is None else [before]
    return pl.pallas_call(
        functools.partial(partial_kernel, place, at, bool(given)),
        in_specs=[VMEM] * (2 + len(given) + len(parts)),
        out_specs=VMEM,
        out_shape=pltpu.VMEM((CA, BS, WIDE), jnp.float32),
        compiler_params=pltpu.CompilerParams(vmem_limit_bytes=16 * MIB),
        cost_estimate=cost(CFG['ca'], 1500),
        name="partial_product",
    )(*map(in_vmem, (high, low, *given, *parts)))


def last_kernel(place, at, out_in_ref, high_ref, low_ref, before_ref, part_ref, out_ref, block, sem):
    del out_in_ref
    block[...] = before_ref[...] + summed(high_ref, low_ref, place, [part_ref], at)
    put_block(groups_here()[place], block, out_ref, sem).wait()


def last_product(out, high, low, before, part, place, at):
    return pl.pallas_call(
        functools.partial(last_kernel, place, at),
        in_specs=[HBM] + [VMEM] * 4,
        out_specs=HBM,
        out_shape=jax.ShapeDtypeStruct(out.shape, out.dtype),
        scratch_shapes=[pltpu.VMEM((CA, BS, WIDE), jnp.float32), pltpu.SemaphoreType.DMA],
        input_output_aliases={0: 0},
        compiler_params=pltpu.CompilerParams(vmem_limit_bytes=16 * MIB),
        cost_estimate=cost(CFG['cz'], 700),
        name="last_product",
    )(out, *map(in_vmem, (high, low, before, part)))


def column_pairs(count):
    return [(i, i ^ 1) for i in range(count)]


def column_onward(count):
    return [(i, ((i ^ 1) + 1) % count if (i ^ 1) % 2 else ((i ^ 1) - 1) % count) for i in range(count)]


def row_pairs(count):
    return [(i, i ^ 1) for i in range(count)]


def row_between(count):
    pairs = [(i, i + 1) for i in range(1, count - 1, 2)]
    return pairs + [(b, a) for a, b in pairs]


def after(value, *others):
    return lax.optimization_barrier((value, *others))[0]


def tick_kernel(value_ref, out_ref):
    out_ref[...] = value_ref[0, :8, :128]


def tick(value, flops):
    return pl.pallas_call(
        tick_kernel,
        in_specs=[VMEM],
        out_specs=VMEM,
        out_shape=pltpu.VMEM((8, 128), jnp.float32),
        cost_estimate=cost(flops, 2000),
        name="tick",
    )(in_vmem(value))


def per_device(a_values, a_columns, p_values, p_columns, p_count, aggregates):
    row_count = lax.axis_size("row")
    col_count = lax.axis_size("col")
    depth = a_values.shape[0] * BS
    pairs, onward = column_pairs(col_count), column_onward(col_count)
    parts, dense = dense_rows(p_values, p_columns, p_count, aggregates)
    pair, far = [], []
    for index, part in enumerate(parts):
        if CFG['xg'] and index >= CFG['xg']:
            part = after(part, pair[index - CFG['xg']])
        pair.append(lax.ppermute(part, "col", pairs))
    own = dense
    if CFG['la'] is not None:
        own = after(dense, pair[CFG['la']])
    cut = CFG['cut']
    rows = a_values.shape[0]
    left = first = left_product(own, a_columns, a_values, None, 0, cut, col_count)
    if cut < rows:
        again = dense if CFG['lb'] is None else after(dense, pair[min(CFG['lb'], len(pair) - 1)])
        left = left_product(again, a_columns, a_values, first, cut, rows - cut, col_count)
    ticked = tick(parts[0], CFG['ck']) if CFG['tick'] else None
    for index, part in enumerate(pair):
        if index in CFG['gf']:
            part = after(part, left)
        if index in CFG['g1']:
            part = after(part, first)
        if CFG['tick'] and index in CFG['gk']:
            part = after(part, ticked)
        far.append(lax.ppermute(part, "col", onward))
    to_row = dense
    if CFG['rg'] == 'left':
        to_row = after(dense, left)
    elif CFG['rg'] == 'tick' and CFG['tick']:
        to_row = after(dense, ticked)
    elif isinstance(CFG['rg'], int):
        to_row = after(dense, pair[CFG['rg']])
    if CFG['rs']:
        pair_row = lax.ppermute(to_row, "row", row_pairs(row_count))
        far_row = lax.ppermute(to_row, "row", row_between(row_count))
    else:
        far_row = lax.ppermute(to_row, "row", row_between(row_count))
        pair_row = lax.ppermute(to_row, "row", row_pairs(row_count))
    high, low = turned(left)
    if CFG['pr'] == 0:
        out = products(None, high, low, {OWN: [dense], PAIR_ROW: [pair_row], FAR_ROW: [far_row], PAIR_COL: pair})
    elif CFG['pr'] == 1:
        out = products(None, high, low, {OWN: [dense], PAIR_ROW: [pair_row], FAR_ROW: [far_row]})
        out = products(out, high, low, {PAIR_COL: pair})
    elif CFG['pr'] == 2:
        out = products(None, high, low, {OWN: [dense], PAIR_COL: pair})
        out = products(out, high, low, {PAIR_ROW: [pair_row], FAR_ROW: [far_row]})
    if CFG['ch']:
        before, at = None, 0
        for part in far[:-1]:
            before = partial_product(high, low, before, [part], FAR_COL, at)
            at += part.shape[0] * BS
    else:
        before = partial_product(high, low, None, far[:-1], FAR_COL, 0)
    return last_product(out, high, low, before, far[-1], FAR_COL, depth - PARTS[-1] * BS)


def solution(mesh):
    in_specs = (
        P(("row", "col"), None, None),
        P(("row", "col"), None),
        P(("row", "col"), None, None),
        P(("row", "col"), None),
        P(("row", "col")),
        P(("row", "col")),
    )
    out_specs = P(("row", "col"), None, None)
    return jax.shard_map(
        per_device, mesh=mesh, in_specs=in_specs, out_specs=out_specs, check_vma=False
    )
```

```python
import functools

import jax
import jax.numpy as jnp
from jax import lax
from jax.experimental import pallas as pl
from jax.experimental.pallas import tpu as pltpu
from jax.sharding import PartitionSpec as P

CFG = {'parts': (2, 3, 3), 'x3': 'f', 'lrc': 1, 'la': 0, 'tick': 1, 'ck': 100000000000, 'gk': (0, 2), 'gr': 'tick', 'gf': (1, 2), 'rg': None, 'cut': 8, 'pr': ((0, 1), (3, 4)), 'fo': (0, 1, 2), 'fl': [1], 'cl': 100000000, 'ct': 1000, 'cp': 100000000, 'ca': 1000000000, 'cz': 100000000}

BS = 64
KA = 7
KP = 4
CA = 4
WIDE = CA * BS
PARTS = CFG['parts']

OWN, PAIR_COL, FAR_COL, PAIR_ROW, FAR_ROW = range(5)

VMEM = pl.BlockSpec(memory_space=pltpu.VMEM)
HBM = pl.BlockSpec(memory_space=pltpu.HBM)
MIB = 1024 * 1024


def split(value):
    high = value.astype(jnp.bfloat16)
    low = (value - high.astype(jnp.float32)).astype(jnp.bfloat16)
    return high, low


def product(high, low, other):
    other_high, other_low = split(other)
    dot = functools.partial(jnp.dot, preferred_element_type=jnp.float32)
    return dot(high, other_high) + (dot(high, other_low) + dot(low, other_high))


def in_hbm(value):
    return pltpu.with_memory_space_constraint(value, pltpu.HBM)


def in_vmem(value):
    return pltpu.with_memory_space_constraint(value, pltpu.VMEM)


def cost(flops, moved):
    return pl.CostEstimate(flops=flops, bytes_accessed=moved, transcendentals=0)


def dense_row(row, values, columns, counts, aggregates):
    lane = lax.broadcasted_iota(jnp.int32, (1, 2 * BS), 1)
    lower = lane < BS
    diagonal = (
        lax.broadcasted_iota(jnp.int32, (BS, 2 * BS), 0)
        == lax.broadcasted_iota(jnp.int32, (BS, 2 * BS), 1) % BS
    ).astype(jnp.float32)
    live = counts[row]
    feeds = [jnp.where(k < live, columns[k, row], -1) for k in range(KP)]
    pieces = []
    for m in range(KP // 2):
        straight = values[:, m * 2 * BS : (m + 1) * 2 * BS]
        pieces.append((jnp.where(lower, feeds[2 * m], feeds[2 * m + 1]), straight))
        pieces.append(
            (jnp.where(lower, feeds[2 * m + 1], feeds[2 * m]), pltpu.roll(straight, BS, 1))
        )
    dense = []
    for j in range(CA // 2):
        wanted = jnp.where(lower, 2 * j, 2 * j + 1)
        total = jnp.where(wanted == aggregates[row], diagonal, 0.0)
        for feed, piece in pieces:
            total = total + jnp.where(feed == wanted, piece, 0.0)
        dense.append(total)
    return jnp.concatenate(dense, axis=1)


def dense_kernel(values_ref, columns_ref, counts_ref, aggregates_ref, *refs):
    count = len(PARTS)
    part_refs = refs[:count]
    dense_ref, values, columns, counts, aggregates, sems = refs[count:]
    small = [
        pltpu.make_async_copy(source, target, sems.at[index])
        for index, (source, target) in enumerate(
            [(columns_ref, columns), (counts_ref, counts), (aggregates_ref, aggregates)]
        )
    ]
    spans = [pl.ds(sum(PARTS[:part]), PARTS[part]) for part in range(count)]
    large = [
        pltpu.make_async_copy(values_ref.at[span], values.at[span], sems.at[3 + part])
        for part, span in enumerate(spans)
    ]
    for copy in small + large:
        copy.start()
    for copy in small:
        copy.wait()
    for part in range(count):
        large[part].wait()
        for index in range(PARTS[part]):
            row = sum(PARTS[:part]) + index
            dense = dense_row(row, values[row], columns, counts, aggregates)
            part_refs[part][index] = dense
            dense_ref[row] = dense


def dense_rows(p_values, p_columns, p_count, aggregates):
    every = p_values.shape[0]
    *parts, dense = pl.pallas_call(
        dense_kernel,
        in_specs=[HBM] * 4,
        out_specs=[VMEM] * (len(PARTS) + 1),
        out_shape=[pltpu.VMEM((rows, BS, WIDE), jnp.float32) for rows in (*PARTS, every)],
        scratch_shapes=[
            pltpu.VMEM(p_values.shape, jnp.float32),
            pltpu.SMEM((KP, every), jnp.int32),
            pltpu.SMEM((every,), jnp.int32),
            pltpu.SMEM((every,), jnp.int32),
            pltpu.SemaphoreType.DMA((3 + len(PARTS),)),
        ],
        cost_estimate=cost(400000, p_values.size * 12),
        name="dense_rows",
    )(in_hbm(p_values), in_hbm(p_columns.T), in_hbm(p_count), in_hbm(aggregates))
    return parts, dense


def put_block(group, block_ref, out_ref, sem):
    at = pl.multiple_of(group * WIDE, WIDE)
    copy = pltpu.make_async_copy(block_ref, out_ref.at[:, :, pl.ds(at, WIDE)], sem)
    copy.start()
    return copy


def left_kernel(col_count, first, dense_ref, columns_ref, a_ref, *refs):
    left, a, columns, sems = refs[-4:]
    rows = dense_ref.shape[0]
    mine = a.shape[0]
    grid_row = lax.axis_index("row")
    grid_col = lax.axis_index("col")
    small = pltpu.make_async_copy(columns_ref, columns, sems.at[0])
    small.start()
    large = [pltpu.make_async_copy(a_ref.at[first + row], a.at[row], sems.at[1 + row]) for row in range(mine)]
    for copy in large:
        copy.start()
    if first == 0:
        left[...] = jnp.zeros_like(left)
    for copy in large:
        copy.wait()
    small.wait()
    for index in range(mine):
        row = first + index
        a_high, a_low = split(a[index])
        p_high, p_low = split(dense_ref[row])
        turned_a = jnp.concatenate([a_high, a_low], axis=0).T
        term = jnp.dot(
            jnp.concatenate([turned_a, turned_a], axis=1),
            jnp.concatenate([p_high, p_high, p_low, p_low], axis=0),
            preferred_element_type=jnp.float32,
        )
        for slot in range(KA):
            target = columns[row, slot]
            sub = target // rows
            sub_row = sub // col_count
            sub_col = sub - sub_row * col_count
            along = jnp.where(sub_col == grid_col, OWN, jnp.where(sub_col == (grid_col ^ 1), PAIR_COL, FAR_COL))
            across = jnp.where(sub_row == (grid_row ^ 1), PAIR_ROW, FAR_ROW)
            group = jnp.where(sub_row == grid_row, along, across)
            at = pl.multiple_of((group * rows + (target - sub * rows)) * BS, BS)
            left[pl.ds(at, BS), :] += term[slot * BS : (slot + 1) * BS]


def left_product(dense, a_columns, a_values, before, first, count, col_count):
    rows = a_values.shape[0]
    given = [] if before is None else [before]
    return pl.pallas_call(
        functools.partial(left_kernel, col_count, first),
        in_specs=[VMEM, HBM, HBM] + [VMEM] * len(given),
        out_specs=VMEM,
        out_shape=pltpu.VMEM((5 * rows * BS, WIDE), jnp.float32),
        scratch_shapes=[
            pltpu.VMEM((count, *a_values.shape[1:]), jnp.float32),
            pltpu.SMEM(a_columns.shape, jnp.int32),
            pltpu.SemaphoreType.DMA((1 + count,)),
        ],
        input_output_aliases={3: 0} if given else {},
        compiler_params=pltpu.CompilerParams(vmem_limit_bytes=16 * MIB),
        cost_estimate=cost(CFG['cl'], 4000),
        name="left_product",
    )(in_vmem(dense), in_hbm(a_columns), in_hbm(a_values), *map(in_vmem, given))


def turn_kernel(left_ref, high_ref, low_ref):
    depth = high_ref.shape[2]
    for place in range(5):
        high_ref[place], low_ref[place] = split(left_ref[place * depth : (place + 1) * depth, :].T)


def turned(left):
    depth = left.shape[0] // 5
    return pl.pallas_call(
        turn_kernel,
        in_specs=[VMEM],
        out_specs=[VMEM, VMEM],
        out_shape=[pltpu.VMEM((5, WIDE, depth), jnp.bfloat16)] * 2,
        compiler_params=pltpu.CompilerParams(vmem_limit_bytes=16 * MIB),
        cost_estimate=cost(CFG['ct'], 5000),
        name="turned",
    )(in_vmem(left))


def groups_here():
    col_odd = lax.axis_index("col") % 2
    row_odd = lax.axis_index("row") % 2
    return {OWN: 0, PAIR_COL: 2 - col_odd, FAR_COL: 1 + col_odd, PAIR_ROW: 4 - row_odd, FAR_ROW: 3 + row_odd}


def summed(high_ref, low_ref, place, part_refs, at=0):
    total = None
    for part_ref in part_refs:
        depth = part_ref.shape[0] * BS
        term = product(
            high_ref[place, :, at : at + depth], low_ref[place, :, at : at + depth], part_ref[...].reshape(depth, WIDE)
        )
        total = term if total is None else total + term
        at += depth
    return total.reshape(CA, BS, WIDE)


def stage_kernel(has_out, flushed, sums, final, *refs):
    refs = list(refs)
    out_in_ref = refs.pop(0) if has_out else None
    del out_in_ref
    high_ref, low_ref = refs.pop(0), refs.pop(0)
    flush_refs = [refs.pop(0) for _ in flushed]
    given = [([refs.pop(0) for _ in range(1 if has_before else 0)], [refs.pop(0) for _ in range(count)]) for _, count, _, has_before in sums]
    out_ref = refs.pop(0) if flushed or final else None
    total_refs = [refs.pop(0) for _ in sums]
    sems = refs.pop(0)
    groups = groups_here()
    copies = [put_block(groups[place], ref, out_ref, sems.at[i]) for i, (place, ref) in enumerate(zip(flushed, flush_refs))]
    for (place, _, at, _), (before, parts), total_ref in zip(sums, given, total_refs):
        total = summed(high_ref, low_ref, place, parts, at)
        total_ref[...] = before[0][...] + total if before else total
        if final:
            copies.append(put_block(groups[place], total_ref, out_ref, sems.at[len(copies)]))
    for copy in copies:
        copy.wait()


def stage(out, high, low, flush, sums, flops, final=False):
    writes = bool(flush) or final
    given_out = [out] if writes and out is not None else []
    shapes = [jax.ShapeDtypeStruct((CA, BS, 5 * WIDE), jnp.float32)] if writes else []
    block = (CA, BS, WIDE)
    flat = list(flush.values())
    for parts, _, before in sums.values():
        flat += ([] if before is None else [before]) + parts
    plan = tuple((place, len(parts), at, before is not None) for place, (parts, at, before) in sums.items())
    scratch = [pltpu.SemaphoreType.DMA((max(1, len(flush) + len(sums)),))]
    if final:
        scratch = [pltpu.VMEM(block, jnp.float32)] * len(sums) + scratch
    else:
        shapes += [pltpu.VMEM(block, jnp.float32)] * len(sums)
    totals = pl.pallas_call(
        functools.partial(stage_kernel, bool(given_out), tuple(flush), plan, final),
        in_specs=[HBM] * len(given_out) + [VMEM] * (2 + len(flat)),
        out_specs=[HBM] * writes + [VMEM] * (len(shapes) - writes),
        out_shape=shapes,
        scratch_shapes=scratch,
        input_output_aliases={0: 0} if given_out else {},
        compiler_params=pltpu.CompilerParams(vmem_limit_bytes=16 * MIB),
        cost_estimate=cost(flops, 2000),
        name="last_product" if final else "stage%d%sf%d" % (len(sums), "p" if plan[0][0] == FAR_COL else "", len(flush)),
    )(*given_out, *map(in_vmem, (high, low, *flat)))
    if writes:
        out, *totals = totals
    return out, dict(zip(sums, totals))


def column_pairs(count):
    return [(i, i ^ 1) for i in range(count)]


def column_onward(count):
    return [(i, ((i ^ 1) + 1) % count if (i ^ 1) % 2 else ((i ^ 1) - 1) % count) for i in range(count)]


def row_pairs(count):
    return [(i, i ^ 1) for i in range(count)]


def beyond(count):
    return [(i, (i + 1) % count if i % 2 else (i - 1) % count) for i in range(count)]


def two_on(count):
    return [(i, (i + 2) % count if i % 2 else (i - 2) % count) for i in range(count)]


def after(value, *others):
    return lax.optimization_barrier((value, *others))[0]


def tick_kernel(value_ref, out_ref):
    out_ref[...] = value_ref[0, :8, :128]


def tick(value, flops):
    return pl.pallas_call(
        tick_kernel,
        in_specs=[VMEM],
        out_specs=VMEM,
        out_shape=pltpu.VMEM((8, 128), jnp.float32),
        cost_estimate=cost(flops, 2000),
        name="tick",
    )(in_vmem(value))


def per_device(a_values, a_columns, p_values, p_columns, p_count, aggregates):
    row_count = lax.axis_size("row")
    col_count = lax.axis_size("col")
    rows = a_values.shape[0]
    pairs, onward = column_pairs(col_count), column_onward(col_count)
    parts, dense = dense_rows(p_values, p_columns, p_count, aggregates)
    ticked = tick(parts[0], CFG['ck']) if CFG['tick'] else None
    direct = lax.ppermute(parts[-1], "col", two_on(col_count))
    to_row = dense
    if CFG['rg'] == 'tick' and CFG['tick']:
        to_row = after(dense, ticked)
    pair_row = lax.ppermute(dense, "row", row_pairs(row_count))
    far_row = lax.ppermute(to_row, "row", beyond(row_count))
    pair = []
    for index, part in enumerate(parts):
        if index == len(parts) - 1 and CFG['x3'] == 'f':
            part = after(part, pair[0])
        elif index == len(parts) - 1 and CFG['x3'] == 'd':
            part = after(part, direct)
        elif index == len(parts) - 1 and CFG['x3'] == 'r':
            part = after(part, pair_row)
        pair.append(lax.ppermute(part, "col", pairs))
    own = dense
    if CFG['lrc']:
        own = after(own, pair_row)
    if CFG['la'] is not None:
        own = after(own, pair[CFG['la']])
    left = left_product(own, a_columns, a_values, None, 0, rows, col_count)
    far = []
    for index, part in enumerate(pair[:-1]):
        if index in CFG['gf']:
            part = after(part, left)
        if CFG['tick'] and index in CFG['gk']:
            part = after(part, ticked)
        far.append(lax.ppermute(part, "col", onward))
    if CFG['gr'] == 'left':
        direct = after(direct, left)
    elif CFG['gr'] == 'tick' and CFG['tick']:
        direct = after(direct, ticked)
    far.append(lax.ppermute(direct, "col", pairs))
    high, low = turned(left)
    given = {OWN: [dense], PAIR_ROW: [pair_row], FAR_ROW: [far_row], PAIR_COL: pair}
    ats = [sum(PARTS[:k]) * BS for k in range(len(PARTS))]
    steps = [{place: (given[place], 0) for place in group} for group in CFG['pr']]
    steps += [{FAR_COL: ([far[k]], ats[k])} for k in CFG['fo']]
    out, ready, before = None, {}, None
    for step, what in enumerate(steps):
        last = step == len(steps) - 1
        now = step in CFG['fl'] or last
        sums = {place: (*some, before if place == FAR_COL else None) for place, some in what.items()}
        flops = CFG['cz'] if last else CFG['ca'] if FAR_COL in what else CFG['cp']
        out, totals = stage(out, high, low, ready if now else {}, sums, flops, last)
        ready = {} if now else ready
        if not last:
            before = totals.pop(FAR_COL, before)
            ready = {**ready, **totals}
    return out


def solution(mesh):
    in_specs = (
        P(("row", "col"), None, None),
        P(("row", "col"), None),
        P(("row", "col"), None, None),
        P(("row", "col"), None),
        P(("row", "col")),
        P(("row", "col")),
    )
    out_specs = P(("row", "col"), None, None)
    return jax.shard_map(
        per_device, mesh=mesh, in_specs=in_specs, out_specs=out_specs, check_vma=False
    )
```

```python
import functools

import jax
import jax.numpy as jnp
from jax import lax
from jax.experimental import pallas as pl
from jax.experimental.pallas import tpu as pltpu
from jax.sharding import PartitionSpec as P

BS = 64
KA = 7
KP = 4
CA = 4
WIDE = CA * BS
PARTS = (2, 3, 3)

OWN, PAIR_COL, FAR_COL, PAIR_ROW, FAR_ROW = range(5)

VMEM = pl.BlockSpec(memory_space=pltpu.VMEM)
HBM = pl.BlockSpec(memory_space=pltpu.HBM)
MIB = 1024 * 1024


def split(value):
    high = value.astype(jnp.bfloat16)
    low = (value - high.astype(jnp.float32)).astype(jnp.bfloat16)
    return high, low


def product(high, low, other):
    other_high, other_low = split(other)
    dot = functools.partial(jnp.dot, preferred_element_type=jnp.float32)
    return dot(high, other_high) + (dot(high, other_low) + dot(low, other_high))


def in_hbm(value):
    return pltpu.with_memory_space_constraint(value, pltpu.HBM)


def in_vmem(value):
    return pltpu.with_memory_space_constraint(value, pltpu.VMEM)


def cost(flops, moved):
    return pl.CostEstimate(flops=flops, bytes_accessed=moved, transcendentals=0)


def dense_row(row, values, columns, counts, aggregates):
    lane = lax.broadcasted_iota(jnp.int32, (1, 2 * BS), 1)
    lower = lane < BS
    diagonal = (
        lax.broadcasted_iota(jnp.int32, (BS, 2 * BS), 0)
        == lax.broadcasted_iota(jnp.int32, (BS, 2 * BS), 1) % BS
    ).astype(jnp.float32)
    live = counts[row]
    feeds = [jnp.where(k < live, columns[k, row], -1) for k in range(KP)]
    pieces = []
    for m in range(KP // 2):
        straight = values[:, m * 2 * BS : (m + 1) * 2 * BS]
        pieces.append((jnp.where(lower, feeds[2 * m], feeds[2 * m + 1]), straight))
        pieces.append(
            (jnp.where(lower, feeds[2 * m + 1], feeds[2 * m]), pltpu.roll(straight, BS, 1))
        )
    dense = []
    for j in range(CA // 2):
        wanted = jnp.where(lower, 2 * j, 2 * j + 1)
        total = jnp.where(wanted == aggregates[row], diagonal, 0.0)
        for feed, piece in pieces:
            total = total + jnp.where(feed == wanted, piece, 0.0)
        dense.append(total)
    return jnp.concatenate(dense, axis=1)


def dense_kernel(values_ref, columns_ref, counts_ref, aggregates_ref, *refs):
    count = len(PARTS)
    part_refs = refs[:count]
    dense_ref, values, columns, counts, aggregates, sems = refs[count:]
    small = [
        pltpu.make_async_copy(source, target, sems.at[index])
        for index, (source, target) in enumerate(
            [(columns_ref, columns), (counts_ref, counts), (aggregates_ref, aggregates)]
        )
    ]
    spans = [pl.ds(sum(PARTS[:part]), PARTS[part]) for part in range(count)]
    large = [
        pltpu.make_async_copy(values_ref.at[span], values.at[span], sems.at[3 + part])
        for part, span in enumerate(spans)
    ]
    for copy in small + large:
        copy.start()
    for copy in small:
        copy.wait()
    for part in range(count):
        large[part].wait()
        for index in range(PARTS[part]):
            row = sum(PARTS[:part]) + index
            dense = dense_row(row, values[row], columns, counts, aggregates)
            part_refs[part][index] = dense
            dense_ref[row] = dense


def dense_rows(p_values, p_columns, p_count, aggregates):
    every = p_values.shape[0]
    *parts, dense = pl.pallas_call(
        dense_kernel,
        in_specs=[HBM] * 4,
        out_specs=[VMEM] * (len(PARTS) + 1),
        out_shape=[pltpu.VMEM((rows, BS, WIDE), jnp.float32) for rows in (*PARTS, every)],
        scratch_shapes=[
            pltpu.VMEM(p_values.shape, jnp.float32),
            pltpu.SMEM((KP, every), jnp.int32),
            pltpu.SMEM((every,), jnp.int32),
            pltpu.SMEM((every,), jnp.int32),
            pltpu.SemaphoreType.DMA((3 + len(PARTS),)),
        ],
        cost_estimate=cost(400000, p_values.size * 12),
        name="dense_rows",
    )(in_hbm(p_values), in_hbm(p_columns.T), in_hbm(p_count), in_hbm(aggregates))
    return parts, dense


def put_block(group, block_ref, out_ref, sem):
    at = pl.multiple_of(group * WIDE, WIDE)
    copy = pltpu.make_async_copy(block_ref, out_ref.at[:, :, pl.ds(at, WIDE)], sem)
    copy.start()
    return copy


def left_kernel(col_count, dense_ref, columns_ref, a_ref, left, a, columns, sems):
    rows = a_ref.shape[0]
    grid_row = lax.axis_index("row")
    grid_col = lax.axis_index("col")
    small = pltpu.make_async_copy(columns_ref, columns, sems.at[0])
    small.start()
    large = [pltpu.make_async_copy(a_ref.at[row], a.at[row], sems.at[1 + row]) for row in range(rows)]
    for copy in large:
        copy.start()
    left[...] = jnp.zeros_like(left)
    for copy in large:
        copy.wait()
    small.wait()
    for row in range(rows):
        a_high, a_low = split(a[row])
        p_high, p_low = split(dense_ref[row])
        turned_a = jnp.concatenate([a_high, a_low], axis=0).T
        term = jnp.dot(
            jnp.concatenate([turned_a, turned_a], axis=1),
            jnp.concatenate([p_high, p_high, p_low, p_low], axis=0),
            preferred_element_type=jnp.float32,
        )
        for slot in range(KA):
            target = columns[row, slot]
            sub = target // rows
            sub_row = sub // col_count
            sub_col = sub - sub_row * col_count
            along = jnp.where(sub_col == grid_col, OWN, jnp.where(sub_col == (grid_col ^ 1), PAIR_COL, FAR_COL))
            across = jnp.where(sub_row == (grid_row ^ 1), PAIR_ROW, FAR_ROW)
            group = jnp.where(sub_row == grid_row, along, across)
            at = pl.multiple_of((group * rows + (target - sub * rows)) * BS, BS)
            left[pl.ds(at, BS), :] += term[slot * BS : (slot + 1) * BS]


def left_product(dense, a_columns, a_values, col_count):
    rows = a_values.shape[0]
    return pl.pallas_call(
        functools.partial(left_kernel, col_count),
        in_specs=[VMEM, HBM, HBM],
        out_specs=VMEM,
        out_shape=pltpu.VMEM((5 * rows * BS, WIDE), jnp.float32),
        scratch_shapes=[
            pltpu.VMEM(a_values.shape, jnp.float32),
            pltpu.SMEM(a_columns.shape, jnp.int32),
            pltpu.SemaphoreType.DMA((1 + rows,)),
        ],
        compiler_params=pltpu.CompilerParams(vmem_limit_bytes=16 * MIB),
        cost_estimate=cost(100000000, 4000),
        name="left_product",
    )(in_vmem(dense), in_hbm(a_columns), in_hbm(a_values))


def turn_kernel(left_ref, high_ref, low_ref):
    depth = high_ref.shape[2]
    for place in range(5):
        high_ref[place], low_ref[place] = split(left_ref[place * depth : (place + 1) * depth, :].T)


def turned(left):
    depth = left.shape[0] // 5
    return pl.pallas_call(
        turn_kernel,
        in_specs=[VMEM],
        out_specs=[VMEM, VMEM],
        out_shape=[pltpu.VMEM((5, WIDE, depth), jnp.bfloat16)] * 2,
        compiler_params=pltpu.CompilerParams(vmem_limit_bytes=16 * MIB),
        cost_estimate=cost(1000, 5000),
        name="turned",
    )(in_vmem(left))


def groups_here():
    col_odd = lax.axis_index("col") % 2
    row_odd = lax.axis_index("row") % 2
    return {OWN: 0, PAIR_COL: 2 - col_odd, FAR_COL: 1 + col_odd, PAIR_ROW: 4 - row_odd, FAR_ROW: 3 + row_odd}


def summed(high_ref, low_ref, place, part_refs, at=0):
    total = None
    for part_ref in part_refs:
        depth = part_ref.shape[0] * BS
        term = product(
            high_ref[place, :, at : at + depth], low_ref[place, :, at : at + depth], part_ref[...].reshape(depth, WIDE)
        )
        total = term if total is None else total + term
        at += depth
    return total.reshape(CA, BS, WIDE)


def stage_kernel(has_out, flushed, sums, final, *refs):
    refs = list(refs)
    out_in_ref = refs.pop(0) if has_out else None
    del out_in_ref
    high_ref, low_ref = refs.pop(0), refs.pop(0)
    flush_refs = [refs.pop(0) for _ in flushed]
    given = [([refs.pop(0) for _ in range(1 if has_before else 0)], [refs.pop(0) for _ in range(count)]) for _, count, _, has_before in sums]
    out_ref = refs.pop(0) if flushed or final else None
    total_refs = [refs.pop(0) for _ in sums]
    sems = refs.pop(0)
    groups = groups_here()
    copies = [put_block(groups[place], ref, out_ref, sems.at[i]) for i, (place, ref) in enumerate(zip(flushed, flush_refs))]
    for (place, _, at, _), (before, parts), total_ref in zip(sums, given, total_refs):
        total = summed(high_ref, low_ref, place, parts, at)
        total_ref[...] = before[0][...] + total if before else total
        if final:
            copies.append(put_block(groups[place], total_ref, out_ref, sems.at[len(copies)]))
    for copy in copies:
        copy.wait()


def stage(out, high, low, flush, sums, flops, final=False):
    writes = bool(flush) or final
    given_out = [out] if writes and out is not None else []
    shapes = [jax.ShapeDtypeStruct((CA, BS, 5 * WIDE), jnp.float32)] if writes else []
    block = (CA, BS, WIDE)
    flat = list(flush.values())
    for parts, _, before in sums.values():
        flat += ([] if before is None else [before]) + parts
    plan = tuple((place, len(parts), at, before is not None) for place, (parts, at, before) in sums.items())
    scratch = [pltpu.SemaphoreType.DMA((max(1, len(flush) + len(sums)),))]
    if final:
        scratch = [pltpu.VMEM(block, jnp.float32)] * len(sums) + scratch
    else:
        shapes += [pltpu.VMEM(block, jnp.float32)] * len(sums)
    totals = pl.pallas_call(
        functools.partial(stage_kernel, bool(given_out), tuple(flush), plan, final),
        in_specs=[HBM] * len(given_out) + [VMEM] * (2 + len(flat)),
        out_specs=[HBM] * writes + [VMEM] * (len(shapes) - writes),
        out_shape=shapes,
        scratch_shapes=scratch,
        input_output_aliases={0: 0} if given_out else {},
        compiler_params=pltpu.CompilerParams(vmem_limit_bytes=16 * MIB),
        cost_estimate=cost(flops, 2000),
        name="last_stage" if final else "stage",
    )(*given_out, *map(in_vmem, (high, low, *flat)))
    if writes:
        out, *totals = totals
    return out, dict(zip(sums, totals))


def column_pairs(count):
    return [(i, i ^ 1) for i in range(count)]


def column_onward(count):
    return [(i, ((i ^ 1) + 1) % count if (i ^ 1) % 2 else ((i ^ 1) - 1) % count) for i in range(count)]


def row_pairs(count):
    return [(i, i ^ 1) for i in range(count)]


def beyond(count):
    return [(i, (i + 1) % count if i % 2 else (i - 1) % count) for i in range(count)]


def two_on(count):
    return [(i, (i + 2) % count if i % 2 else (i - 2) % count) for i in range(count)]


def after(value, *others):
    return lax.optimization_barrier((value, *others))[0]


def mark_kernel(value_ref, out_ref):
    out_ref[...] = value_ref[0, :8, :128]


def mark(value, flops):
    return pl.pallas_call(
        mark_kernel,
        in_specs=[VMEM],
        out_specs=VMEM,
        out_shape=pltpu.VMEM((8, 128), jnp.float32),
        cost_estimate=cost(flops, 2000),
        name="mark",
    )(in_vmem(value))


def per_device(a_values, a_columns, p_values, p_columns, p_count, aggregates):
    row_count = lax.axis_size("row")
    col_count = lax.axis_size("col")
    pairs, onward = column_pairs(col_count), column_onward(col_count)
    parts, dense = dense_rows(p_values, p_columns, p_count, aggregates)
    started = mark(parts[0], 100000000000)
    direct = lax.ppermute(parts[-1], "col", two_on(col_count))
    pair_row = lax.ppermute(dense, "row", row_pairs(row_count))
    far_row = lax.ppermute(dense, "row", beyond(row_count))
    pair = [lax.ppermute(part, "col", pairs) for part in parts[:-1]]
    pair.append(lax.ppermute(after(parts[-1], pair[0]), "col", pairs))
    left = left_product(after(after(dense, pair_row), pair[0]), a_columns, a_values, col_count)
    far = [lax.ppermute(after(pair[0], started), "col", onward)]
    far.append(lax.ppermute(after(pair[1], left), "col", onward))
    far.append(lax.ppermute(after(direct, started), "col", pairs))
    high, low = turned(left)
    places = {OWN: [dense], PAIR_COL: pair}, {PAIR_ROW: [pair_row], FAR_ROW: [far_row]}
    _, ready = stage(None, high, low, {}, {place: (whole, 0, None) for place, whole in places[0].items()}, 100000000)
    out, blocks = stage(None, high, low, ready, {place: (whole, 0, None) for place, whole in places[1].items()}, 100000000)
    at, before = 0, None
    for part in far[:-1]:
        _, totals = stage(None, high, low, {}, {FAR_COL: ([part], at, before)}, 1000000000)
        at, before = at + part.shape[0] * BS, totals[FAR_COL]
    return stage(out, high, low, blocks, {FAR_COL: ([far[-1]], at, before)}, 100000000, True)[0]


def solution(mesh):
    in_specs = (
        P(("row", "col"), None, None),
        P(("row", "col"), None),
        P(("row", "col"), None, None),
        P(("row", "col"), None),
        P(("row", "col")),
        P(("row", "col")),
    )
    out_specs = P(("row", "col"), None, None)
    return jax.shard_map(
        per_device, mesh=mesh, in_specs=in_specs, out_specs=out_specs, check_vma=False
    )
```
